32 devices in a mesh: shard: 8 (over z, y), tensor: 4 (over x, core).
Axes of the slice: x: 2, y: 2, z: 4, core: 2. Of those that a mesh axis runs over, the one named last changes fastest.
Arguments:
- inputs: bfloat16 [8192, 768], P(('shard', 'tensor')), may hold values from -6 to 6
- w_query: bfloat16 [768, 768], P('shard', 'tensor'), may hold values from -0.21875 to 0.21875
- w_key: bfloat16 [768, 768], P('shard', 'tensor'), may hold values from -0.21875 to 0.21875
- w_value: bfloat16 [768, 768], P('shard', 'tensor'), may hold values from -0.21875 to 0.21875
- bias_query: float32 [768], replicated, may hold values from -1 to 1
- bias_value: float32 [768], replicated, may hold values from -0.1 to 0.1
- w_out: bfloat16 [768, 768], P('tensor', 'shard'), may hold values from -4 to 4
- bias_out: float32 [768], replicated, may hold values from -1.5 to 1.5
- gain_one: float32 [768], replicated, may hold values from 0.5 to 1.5
- shift_one: float32 [768], replicated, may hold values from -1 to 1
- gain_two: float32 [768], replicated, may hold values from 0.5 to 1.5
- shift_two: float32 [768], replicated, may hold values from -1 to 1
- w_up: bfloat16 [768, 3072], P('shard', 'tensor'), may hold values from -0.21875 to 0.21875
- bias_up: float32 [3072], replicated, may hold values from -1.5 to 1.5
- w_down: bfloat16 [3072, 768], P('tensor', 'shard'), may hold values from -0.109375 to 0.109375
- bias_down: float32 [768], replicated, may hold values from -1.5 to 1.5
- cotangent: bfloat16 [8192, 768], P(('shard', 'tensor')), may hold values from -6 to 6
Outputs:
- output: float32 [8192, 768], P(('shard', 'tensor'))
- grad_inputs: float32 [8192, 768], P(('shard', 'tensor'))
- grad_w_query: float32 [768, 768], P('shard', 'tensor')
- grad_w_key: float32 [768, 768], P('shard', 'tensor')
- grad_w_value: float32 [768, 768], P('shard', 'tensor')
- grad_bias_query: float32 [768], replicated
- grad_bias_value: float32 [768], replicated
- grad_w_out: float32 [768, 768], P('tensor', 'shard')
- grad_bias_out: float32 [768], replicated
- grad_gain_one: float32 [768], replicated
- grad_shift_one: float32 [768], replicated
- grad_gain_two: float32 [768], replicated
- grad_shift_two: float32 [768], replicated
- grad_w_up: float32 [768, 3072], P('shard', 'tensor')
- grad_bias_up: float32 [3072], replicated
- grad_w_down: float32 [3072, 768], P('tensor', 'shard')
- grad_bias_down: float32 [768], replicated
The draws below stay inside these ranges and needn't reach their ends.
All inputs are finite; a program needn't handle non-finite values.
Results may differ from the reference program's by a relative error of at most 0.02.
Values may be sent and summed in bfloat16 or wider, within the bound.
A program may use at most 128 MiB of HBM per device.

```python
import math
import jax
import jax.numpy as jnp
from jax import lax

D = 768
HEADS = 12
HD = 64
FF = 3072
LENGTH = 1024
CLIPS = 8
TOKENS = 8192
N_TENSOR = 4


def shard_levels(rng, extent, cuts, low, largest):
    loudness, own = 1.0, jax.random.fold_in(rng, 6)
    for dim, blocks in cuts:
        steps = jnp.exp(jax.random.uniform(jax.random.fold_in(own, dim), (blocks,), jnp.float32, low / len(cuts), largest / len(cuts)))
        loudness = loudness * jnp.repeat(steps, extent[dim] // blocks).reshape([-1 if axis == dim else 1 for axis in range(len(extent))])
    return loudness


def bell_draw(own_key, dims, deviation, bound, shards=(), kind=jnp.bfloat16):
    values = deviation * jax.random.normal(own_key, dims, jnp.float32)
    if shards:
        values = values * shard_levels(own_key, dims, shards, -0.22, 0.18)
    return jnp.clip(values, -bound, bound).astype(kind)


def setup_inputs(seed: int = 0) -> dict:
    seeds = jax.random.split(jax.random.key(seed), 18)
    inputs = bell_draw(seeds[0], (TOKENS, D), 1.0, 6.0, ((0, 32),))
    w_query = bell_draw(seeds[1], (D, D), D ** -0.5, 0.21875, ((0, 8), (1, 4)))
    w_key = bell_draw(seeds[2], (D, D), D ** -0.5, 0.21875, ((0, 8), (1, 4)))
    w_value = bell_draw(seeds[3], (D, D), D ** -0.5, 0.21875, ((0, 8), (1, 4)))
    bias_query = bell_draw(seeds[4], (D,), 0.2, 1.0, (), jnp.float32)
    bias_value = bell_draw(seeds[5], (D,), 0.02, 0.1, (), jnp.float32)
    w_out = bell_draw(seeds[6], (D, D), (max(3 * D // LENGTH, 1)) ** -0.5, 4.0, ((0, 4), (1, 8)))
    bias_out = bell_draw(seeds[7], (D,), 0.3, 1.5, (), jnp.float32)
    gain_one = jnp.clip(1.0 + 0.1 * jax.random.normal(seeds[8], (D,), jnp.float32), 0.5, 1.5)
    shift_one = bell_draw(seeds[9], (D,), 0.2, 1.0, (), jnp.float32)
    gain_two = jnp.clip(1.0 + 0.1 * jax.random.normal(seeds[10], (D,), jnp.float32), 0.5, 1.5)
    shift_two = bell_draw(seeds[11], (D,), 0.2, 1.0, (), jnp.float32)
    w_up = bell_draw(seeds[12], (D, FF), D ** -0.5, 0.21875, ((0, 8), (1, 4)))
    bias_up = bell_draw(seeds[13], (FF,), 0.3, 1.5, (), jnp.float32)
    w_down = bell_draw(seeds[14], (FF, D), FF ** -0.5, 0.109375, ((0, 4), (1, 8)))
    bias_down = bell_draw(seeds[15], (D,), 0.3, 1.5, (), jnp.float32)
    cotangent = bell_draw(seeds[16], (TOKENS, D), 1.0, 6.0, ((0, 32),))
    return {"inputs": inputs, "w_query": w_query, "w_key": w_key, "w_value": w_value, "bias_query": bias_query, "bias_value": bias_value, "w_out": w_out, "bias_out": bias_out, "gain_one": gain_one, "shift_one": shift_one, "gain_two": gain_two, "shift_two": shift_two, "w_up": w_up, "bias_up": bias_up, "w_down": w_down, "bias_down": bias_down, "cotangent": cotangent}


epsilon = 1e-05
highest = lax.Precision.HIGHEST

@jax.custom_vjp
def low(v):
    return lax.optimization_barrier(v.astype(jnp.bfloat16)).astype(jnp.float32)

@jax.custom_vjp
def low_back(v):
    return v

def low_keep(v):
    return (low(v), None)

def low_pass(kept, grad):
    return (grad,)

def back_keep(v):
    return (v, None)

def back_low(kept, grad):
    return (low(grad),)
low.defvjp(low_keep, low_pass)
low_back.defvjp(back_keep, back_low)

def layer_norm(matrix, gain_vec, shift_vec):
    center = matrix - lax.optimization_barrier(jnp.mean(matrix, axis=-1, keepdims=True))
    return center * lax.rsqrt(lax.optimization_barrier(jnp.mean(center * center, axis=-1, keepdims=True)) + epsilon) * gain_vec + shift_vec

def matmul(left_side, right_side):
    return jnp.dot(left_side, right_side, precision=highest)

def attend(queries, key_rows, value_rows):
    length = queries.shape[0]
    block_rows = min(512, length)
    score_scale = 1.0 / math.sqrt(queries.shape[2])
    blocks = queries.reshape(length // block_rows, block_rows, queries.shape[1], queries.shape[2])

    def one_block(query_block):
        scores = low_back(jnp.einsum('qhd,khd->hqk', query_block, key_rows, precision=highest)) * score_scale
        soft_low = low(jax.nn.softmax(scores, axis=-1))
        return jnp.einsum('hqk,khd->qhd', soft_low, value_rows, precision=highest)
    mixture = lax.map(jax.checkpoint(one_block), blocks)
    return mixture.reshape(length, queries.shape[1] * queries.shape[2])

def clip_layer(frames, params):
    w_query, w_key, w_value, bias_query, bias_value, w_out, bias_out, gain_one, shift_one, gain_two, shift_two, w_up, bias_up, w_down, bias_down = params
    heads_each = HEADS // N_TENSOR
    head_cols = heads_each * HD
    unit_count = FF // N_TENSOR
    normed_one = low(layer_norm(frames, gain_one, shift_one))
    branch_one = jnp.zeros_like(frames)
    for member in range(N_TENSOR):
        offset = member * head_cols
        shared = low_back(normed_one)
        queries = low(low_back(matmul(shared, w_query[:, offset:offset + head_cols])) + bias_query[offset:offset + head_cols])
        key_rows = low(low_back(matmul(shared, w_key[:, offset:offset + head_cols])))
        value_rows = low(low_back(matmul(shared, w_value[:, offset:offset + head_cols])) + bias_value[offset:offset + head_cols])
        attended = low(low_back(attend(queries.reshape(LENGTH, heads_each, HD), key_rows.reshape(LENGTH, heads_each, HD), value_rows.reshape(LENGTH, heads_each, HD))))
        branch_one = branch_one + low(matmul(attended, w_out[offset:offset + head_cols, :]))
    hidden_state = frames + low_back(branch_one) + bias_out
    normed_two = low(layer_norm(hidden_state, gain_two, shift_two))
    branch_two = jnp.zeros_like(frames)
    for member in range(N_TENSOR):
        offset = member * unit_count
        shared = low_back(normed_two)
        pre_act = low_back(matmul(shared, w_up[:, offset:offset + unit_count])) + bias_up[offset:offset + unit_count]
        activated = low(jax.nn.gelu(pre_act, approximate=False))
        branch_two = branch_two + low(matmul(activated, w_down[offset:offset + unit_count, :]))
    return hidden_state + low_back(branch_two) + bias_down

def reference(inputs, w_query, w_key, w_value, bias_query, bias_value, w_out, bias_out, gain_one, shift_one, gain_two, shift_two, w_up, bias_up, w_down, bias_down, cotangent):
    params = tuple((argument.astype(jnp.float32) for argument in (w_query, w_key, w_value, bias_query, bias_value, w_out, bias_out, gain_one, shift_one, gain_two, shift_two, w_up, bias_up, w_down, bias_down)))
    frames_all = inputs.astype(jnp.float32).reshape(CLIPS, LENGTH, D)
    layer_saved = jax.checkpoint(clip_layer)

    def forward(frames_all, params):

        def per_clip(carried, frames):
            return (carried, layer_saved(frames, params))
        _, outputs = lax.scan(per_clip, jnp.zeros((), jnp.float32), frames_all)
        return outputs
    output, pullback = jax.vjp(forward, frames_all, params)
    grad_frames, grad_params = pullback(cotangent.astype(jnp.float32).reshape(CLIPS, LENGTH, D))
    return (output.reshape(TOKENS, D), grad_frames.reshape(TOKENS, D), grad_params[0], grad_params[1], grad_params[2], grad_params[3], grad_params[4], grad_params[5], grad_params[6], grad_params[7], grad_params[8], grad_params[9], grad_params[10], grad_params[11], grad_params[12], grad_params[13], grad_params[14])
```

```python
import functools
import math

import jax
import jax.numpy as jnp
from jax import lax
from jax.experimental import pallas as pl
from jax.experimental.pallas import tpu as pltpu
from jax.sharding import PartitionSpec as P

HD = 64
MESH = pl.DeviceIdType.MESH
F32 = jnp.float32
BF16 = jnp.bfloat16

epsilon = 1e-05


def normalize(matrix, gain_vec, shift_vec):
    center = matrix - jnp.mean(matrix, axis=1, keepdims=True)
    inverse = lax.rsqrt(jnp.mean(center * center, axis=1, keepdims=True) + epsilon)
    unit_rows = center * inverse
    return (unit_rows * gain_vec + shift_vec, unit_rows, inverse)


def norm_backward(grad_normed, unit_rows, inverse, gain_vec):
    grad_unit = grad_normed * gain_vec
    first_mean = jnp.mean(grad_unit, axis=1, keepdims=True)
    second_mean = jnp.mean(grad_unit * unit_rows, axis=1, keepdims=True)
    grad_rows = inverse * (grad_unit - first_mean - unit_rows * second_mean)
    return (grad_rows, jnp.sum(grad_normed * unit_rows, axis=0), jnp.sum(grad_normed, axis=0))


def exact_gelu(values):
    return jax.nn.gelu(values, approximate=False)


def flip(index, bit):
    return index + bit - 2 * bit * lax.rem(lax.div(index, bit), 2)


def greet(tensor_peers, shard_peers):
    barrier = pltpu.get_barrier_semaphore()
    for peer in tensor_peers:
        pl.semaphore_signal(barrier, inc=1, device_id={"tensor": peer}, device_id_type=MESH)
    for peer in shard_peers:
        pl.semaphore_signal(barrier, inc=1, device_id={"shard": peer}, device_id_type=MESH)
    pl.semaphore_wait(barrier, len(tensor_peers) + len(shard_peers))


def shard_peers_of(me, count):
    return [flip(me, 1)] + [lax.rem(me + 2 * step, count) for step in range(1, count // 2)]


class Tally:
    def __init__(self, send, recv):
        self.send, self.recv, self.used, self.sent = send, recv, 0, []

    def copy(self, source, target, **peer):
        slot = self.used
        self.used += 1
        made = pltpu.make_async_remote_copy(
            src_ref=source,
            dst_ref=target,
            send_sem=self.send.at[slot],
            recv_sem=self.recv.at[slot],
            device_id=peer,
            device_id_type=MESH,
        )
        made.start()
        self.sent.append(made)
        return made

    def finish(self):
        for made in self.sent:
            made.wait_send()


def halves(rows, parts=2):
    size = rows // parts
    return [pl.ds(part * size, size) for part in range(parts)]


def tensor_gather_start(tally, blocks, tensor):
    rows = blocks.shape[1]
    far = [
        tally.copy(blocks.at[tensor, cut], blocks.at[tensor, cut], tensor=flip(tensor, 2))
        for cut in halves(rows)
    ]
    near = [tally.copy(blocks.at[tensor], blocks.at[tensor], tensor=flip(tensor, 1))]
    return far, near


def tensor_gather_end(tally, blocks, tensor, state):
    far, near = state
    rows = blocks.shape[1]
    other = flip(tensor, 2)
    for arrived, cut in zip(far, halves(rows)):
        arrived.wait_recv()
        near.append(
            tally.copy(blocks.at[other, cut], blocks.at[other, cut], tensor=flip(tensor, 1))
        )
    for arrived in near:
        arrived.wait_recv()


def tensor_sum_start(tally, parts, landed, tensor):
    sibling, far = flip(tensor, 1), flip(tensor, 2)
    rows = parts.shape[1]
    passing = [
        tally.copy(parts.at[flip(sibling, 2), cut], landed.at[1, cut], tensor=sibling)
        for cut in halves(rows)
    ]
    own = tally.copy(parts.at[sibling], landed.at[0], tensor=sibling)
    return passing, own


def tensor_sum_pass(tally, parts, landed, mixed, tensor, state):
    far = flip(tensor, 2)
    rows = parts.shape[1]
    across = []
    for arrived, cut in zip(state[0], halves(rows)):
        arrived.wait_recv()
        mixed[cut, :] = (parts[far, cut, :].astype(F32) + landed[1, cut, :].astype(F32)).astype(
            BF16
        )
        across.append(tally.copy(mixed.at[cut], landed.at[2, cut], tensor=far))
    return across


def tensor_sum_end(parts, landed, tensor, state, across):
    state[1].wait_recv()
    for arrived in across:
        arrived.wait_recv()
    return parts[tensor].astype(F32) + landed[0].astype(F32) + landed[2].astype(F32)


def gather_kernel(count, *refs):
    (x_ref, gain_ref, shift_ref, cot_ref, w_refs, rows_ref, cots_ref, full_refs, send, recv,
     local) = (refs[0], refs[1], refs[2], refs[3], refs[4:7], refs[7], refs[8], refs[9:12],
               refs[12], refs[13], refs[14])
    tensor, shard = lax.axis_index("tensor"), lax.axis_index("shard")
    partner = flip(shard, 1)
    peers = shard_peers_of(shard, count)
    greet([flip(tensor, 1), flip(tensor, 2)], peers)
    tally = Tally(send, recv)
    keeps = []
    for place, (w_ref, full) in enumerate(zip(w_refs, full_refs)):
        keep = pltpu.make_async_copy(w_ref, full.at[shard], local.at[place])
        keep.start()
        keeps.append(keep)
    keep = pltpu.make_async_copy(cot_ref, cots_ref.at[tensor], local.at[3])
    keep.start()
    keeps.append(keep)
    straight, beside = [], []

    def send_own(place):
        w_ref, full = w_refs[place], full_refs[place]
        straight.append([
            tally.copy(w_ref, full.at[shard], shard=peer) for peer in peers[1:]
        ])
        beside.append(tally.copy(w_ref, full.at[shard], shard=partner))

    send_own(0)
    rows_ref[tensor] = normalize(x_ref[...].astype(F32), gain_ref[...], shift_ref[...])[0].astype(
        BF16
    )
    rows_state = tensor_gather_start(tally, rows_ref, tensor)
    send_own(1)
    send_own(2)
    for keep in keeps:
        keep.wait()
    cot_state = tensor_gather_start(tally, cots_ref, tensor)
    tensor_gather_end(tally, rows_ref, tensor, rows_state)
    passed = []
    for place in range(3):
        full = full_refs[place]
        for step in range(1, count // 2):
            straight[place][step - 1].wait_recv()
            origin = lax.rem(shard + count - 2 * step, count)
            passed.append(tally.copy(full.at[origin], full.at[origin], shard=partner))
    tensor_gather_end(tally, cots_ref, tensor, cot_state)
    for arrived in beside + passed:
        arrived.wait_recv()
    tally.finish()


def middle_kernel(parts_ref, x_ref, bias_ref, gain_ref, shift_ref, hidden_ref, rows_ref,
                  landed, mixed, send, recv):
    tensor = lax.axis_index("tensor")
    greet([flip(tensor, 1), flip(tensor, 2)], [])
    tally = Tally(send, recv)
    state = tensor_sum_start(tally, parts_ref, landed, tensor)
    across = tensor_sum_pass(tally, parts_ref, landed, mixed, tensor, state)
    branch = tensor_sum_end(parts_ref, landed, tensor, state, across)
    hidden = x_ref[...].astype(F32) + branch + bias_ref[...]
    hidden_ref[...] = hidden
    rows_ref[tensor] = normalize(hidden, gain_ref[...], shift_ref[...])[0].astype(BF16)
    rows_state = tensor_gather_start(tally, rows_ref, tensor)
    tensor_gather_end(tally, rows_ref, tensor, rows_state)
    tally.finish()


def turn_kernel(parts_ref, hidden_ref, cot_ref, gain_ref, grad_ref, rows_ref, small_ref,
                landed, mixed, send, recv):
    tensor = lax.axis_index("tensor")
    greet([flip(tensor, 1), flip(tensor, 2)], [])
    tally = Tally(send, recv)
    state = tensor_sum_start(tally, parts_ref, landed, tensor)
    across = tensor_sum_pass(tally, parts_ref, landed, mixed, tensor, state)
    _, unit, inverse = normalize(hidden_ref[...], gain_ref[...], gain_ref[...])
    normed = tensor_sum_end(parts_ref, landed, tensor, state, across)
    grad_rows, grad_gain, grad_shift = norm_backward(normed, unit, inverse, gain_ref[...])
    cot = cot_ref[...].astype(F32)
    grad = cot + grad_rows
    grad_ref[...] = grad
    rows_ref[tensor] = grad.astype(BF16)
    rows_state = tensor_gather_start(tally, rows_ref, tensor)
    small_ref[0:1, :] = grad_gain.reshape(1, -1)
    small_ref[1:2, :] = grad_shift.reshape(1, -1)
    small_ref[2:3, :] = jnp.sum(grad, axis=0, keepdims=True)
    small_ref[3:4, :] = jnp.sum(cot, axis=0, keepdims=True)
    small_ref[4:8, :] = jnp.zeros((4, small_ref.shape[1]), F32)
    tensor_gather_end(tally, rows_ref, tensor, rows_state)
    tally.finish()


def shard_sum_start(tally, grads, ybufs, shard, count):
    half = count // 2
    place = lax.div(shard, 2)
    low = lax.rem(shard, 2)
    sent = []
    for step in list(range(1, half)) + [0]:
        pair = lax.rem(place + step, half)
        row = []
        for grad, ybuf in zip(grads, ybufs):
            row.append(
                tally.copy(grad.at[pair * 2 + 1 - low], ybuf.at[step], shard=flip(shard, 1))
            )
        sent.append((step, row))
    return sent


def shard_sum_pass(tally, grads, ybufs, zbufs, shard, count, sent):
    half = count // 2
    place = lax.div(shard, 2)
    low = lax.rem(shard, 2)
    across = []
    for step, row in sent:
        pair = lax.rem(place + step, half)
        for grad, ybuf, zbuf, arrived in zip(grads, ybufs, zbufs, row):
            arrived.wait_recv()
            if step:
                ybuf[step] = (
                    grad[pair * 2 + low].astype(F32) + ybuf[step].astype(F32)
                ).astype(BF16)
                across.append(
                    tally.copy(ybuf.at[step], zbuf.at[step], shard=pair * 2 + low)
                )
    return across


def shard_sum_end(grads, ybufs, zbufs, outs, shard, count, across):
    for arrived in across:
        arrived.wait_recv()
    for grad, ybuf, zbuf, out in zip(grads, ybufs, zbufs, outs):
        total = grad[shard].astype(F32) + ybuf[0].astype(F32)
        for step in range(1, count // 2):
            total = total + zbuf[step].astype(F32)
        out[...] = total


def last_kernel(count, two_ref, one_ref, hidden_ref, bias_ref, x_ref, gain_ref, grad_ref,
                small_ref, g0, g1, g2, output_ref, inputs_ref, o0, o1, o2, total_ref,
                landed2, mixed2, landed1, mixed1, y0, y1, y2, z0, z1, z2,
                mine, sums_t, sums_s, sums_g, send, recv):
    tensor, shard = lax.axis_index("tensor"), lax.axis_index("shard")
    near, far = flip(tensor, 1), flip(tensor, 2)
    partner = flip(shard, 1)
    peers = shard_peers_of(shard, count)
    greet([near, far, flip(near, 2)], peers)
    tally = Tally(send, recv)
    grads, ybufs, zbufs = (g0, g1, g2), (y0, y1, y2), (z0, z1, z2)
    sent = shard_sum_start(tally, grads, ybufs, shard, count)
    one_state = tensor_sum_start(tally, one_ref, landed1, tensor)
    two_state = tensor_sum_start(tally, two_ref, landed2, tensor)
    one_across = tensor_sum_pass(tally, one_ref, landed1, mixed1, tensor, one_state)
    two_across = tensor_sum_pass(tally, two_ref, landed2, mixed2, tensor, two_state)
    across = shard_sum_pass(tally, grads, ybufs, zbufs, shard, count, sent)
    _, unit, inverse = normalize(x_ref[...].astype(F32), gain_ref[...], gain_ref[...])
    normed = tensor_sum_end(one_ref, landed1, tensor, one_state, one_across)
    grad_rows, grad_gain, grad_shift = norm_backward(normed, unit, inverse, gain_ref[...])
    mine[0:6, :] = small_ref[0:6, :]
    mine[6:7, :] = grad_gain.reshape(1, -1)
    mine[7:8, :] = grad_shift.reshape(1, -1)
    half = count // 2
    first = tally.copy(mine, sums_s.at[0], shard=partner)
    inputs_ref[...] = grad_ref[...] + grad_rows
    first.wait_recv()
    sums_t[...] = mine[...] + sums_s[0]
    hops = [
        tally.copy(sums_t, sums_s.at[step], shard=lax.rem(shard + 2 * step, count))
        for step in range(1, half)
    ]
    branch = tensor_sum_end(two_ref, landed2, tensor, two_state, two_across)
    output_ref[...] = hidden_ref[...] + branch + bias_ref[...]
    for hop in hops:
        hop.wait_recv()
    slot_total = None
    for spot in range(half):
        step = lax.rem(lax.div(shard, 2) + half - spot, half)
        value = jnp.where(step == 0, sums_t[...], sums_s[step])
        slot_total = value if slot_total is None else slot_total + value
    sums_g[tensor] = slot_total
    spread = [
        tally.copy(sums_g.at[tensor], sums_g.at[tensor], tensor=peer)
        for peer in (near, far, flip(near, 2))
    ]
    shard_sum_end(grads, ybufs, zbufs, (o0, o1, o2), shard, count, across)
    for arrived in spread:
        arrived.wait_recv()
    total_ref[...] = sums_g[...]
    tally.finish()


def attend_kernel(heads, scale, qkv_ref, out_ref):
    length = qkv_ref.shape[0]
    width = heads * HD
    size = min(256, length)

    def block(step, carry):
        rows = pl.ds(pl.multiple_of(step * size, size), size)
        mixed = []
        for head in range(heads):
            query = qkv_ref[rows, head * HD:(head + 1) * HD]
            keys = qkv_ref[:, width + head * HD:width + (head + 1) * HD]
            values = qkv_ref[:, 2 * width + head * HD:2 * width + (head + 1) * HD]
            scores = lax.dot_general(
                query, keys, (((1,), (1,)), ((), ())), preferred_element_type=F32
            ) * scale
            exponent = jnp.exp(scores - jnp.max(scores, axis=1, keepdims=True))
            soft = (exponent * (1.0 / jnp.sum(exponent, axis=1, keepdims=True))).astype(BF16)
            mixed.append(jnp.dot(soft, values, preferred_element_type=F32))
        out_ref[rows, :] = jnp.concatenate(mixed, axis=1).astype(BF16)
        return carry

    lax.fori_loop(0, length // size, block, 0)


def attend_back_kernel(heads, scale, qkv_ref, grad_ref, low_ref, bias_ref, dq, dk, dv):
    length = qkv_ref.shape[0]
    width = heads * HD
    size = min(256, length)
    dk[...] = jnp.zeros_like(dk)
    dv[...] = jnp.zeros_like(dv)

    def block(step, carry):
        rows = pl.ds(pl.multiple_of(step * size, size), size)
        back = []
        for head in range(heads):
            query = qkv_ref[rows, head * HD:(head + 1) * HD]
            keys = qkv_ref[:, width + head * HD:width + (head + 1) * HD]
            values = qkv_ref[:, 2 * width + head * HD:2 * width + (head + 1) * HD]
            grad = grad_ref[rows, head * HD:(head + 1) * HD]
            scores = lax.dot_general(
                query, keys, (((1,), (1,)), ((), ())), preferred_element_type=F32
            ) * scale
            exponent = jnp.exp(scores - jnp.max(scores, axis=1, keepdims=True))
            soft = exponent * (1.0 / jnp.sum(exponent, axis=1, keepdims=True))
            grad_soft = lax.dot_general(
                grad, values, (((1,), (1,)), ((), ())), preferred_element_type=F32
            )
            inner = jnp.sum(grad_soft * soft, axis=1, keepdims=True)
            grad_scores = (soft * (grad_soft - inner) * scale).astype(BF16)
            back.append(jnp.dot(grad_scores, keys, preferred_element_type=F32))
            dk[head] += lax.dot_general(
                query, grad_scores, (((0,), (0,)), ((), ())), preferred_element_type=F32
            )
            dv[head] += lax.dot_general(
                grad, soft.astype(BF16), (((0,), (0,)), ((), ())), preferred_element_type=F32
            )
        dq[rows, :] = jnp.concatenate(back, axis=1)
        return carry

    lax.fori_loop(0, length // size, block, 0)
    key_rows = jnp.concatenate([dk[head] for head in range(heads)], axis=0).T
    value_rows = jnp.concatenate([dv[head] for head in range(heads)], axis=0).T
    query_rows = dq[...]
    low_ref[...] = jnp.concatenate([query_rows, key_rows, value_rows], axis=1).astype(BF16)
    bias_ref[...] = jnp.concatenate(
        [jnp.sum(query_rows, axis=0, keepdims=True), jnp.sum(value_rows, axis=0, keepdims=True)],
        axis=1,
    )


VM = pl.BlockSpec(memory_space=pltpu.VMEM)
HB = pl.BlockSpec(memory_space=pl.ANY)


def call(kernel, ins, outs, scratch, operands, name, collective=None):
    remote = collective is not None
    return pl.pallas_call(
        kernel,
        out_shape=list(outs),
        in_specs=ins,
        out_specs=[VM] * len(outs),
        scratch_shapes=scratch,
        compiler_params=pltpu.CompilerParams(
            vmem_limit_bytes=56 * 2**20,
            **(dict(collective_id=collective, has_side_effects=True) if remote else {}),
        ),
        name=name,
    )(*operands)


def dma(count):
    return [pltpu.SemaphoreType.DMA((count,)), pltpu.SemaphoreType.DMA((count,))]


def shape(dims, kind=BF16):
    return jax.ShapeDtypeStruct(tuple(dims), kind)


def shards(
    inputs, w_query, w_key, w_value, bias_query, bias_value, w_out, bias_out, gain_one,
    shift_one, gain_two, shift_two, w_up, bias_up, w_down, bias_down, cotangent,
):
    count, tensors = lax.axis_size("shard"), lax.axis_size("tensor")
    tensor = lax.axis_index("tensor")
    frames_here, width = inputs.shape
    length = frames_here * tensors
    cols = w_query.shape[1]
    heads = cols // HD
    units = w_up.shape[1]
    scale = 1.0 / math.sqrt(HD)
    rows = w_query.shape[0]
    padded = -(-rows // 16) * 16
    row = lambda vector: vector.reshape(1, -1)
    pad = lambda block: jnp.pad(block, ((0, padded - rows), (0, 0)))
    join = lambda blocks: blocks[:, :rows].reshape(count * rows, blocks.shape[2])
    split = lambda whole: jnp.pad(
        whole.reshape(count, rows, whole.shape[1]), ((0, 0), (0, padded - rows), (0, 0))
    )
    w_attend = jnp.concatenate([w_query, w_key, w_value, w_out.T], axis=1)
    wide = w_attend.shape[1]
    block = (tensors, frames_here, width)

    n_copies = 6 + 2 * 5 + 3 * count
    rows_one, cots, full_attend, full_up, full_down = call(
        functools.partial(gather_kernel, count),
        [VM] * 7,
        [shape(block), shape(block), shape((count, padded, wide)),
         shape((count, padded, units)), shape((count, padded, units))],
        dma(n_copies) + [pltpu.SemaphoreType.DMA((4,))],
        (inputs, row(gain_one), row(shift_one), cotangent, pad(w_attend), pad(w_up),
         pad(w_down.T)),
        "gather_all", 0,
    )
    rows_one = rows_one.reshape(length, width)
    cots = cots.reshape(length, width)
    full_attend, full_up, full_down = join(full_attend), join(full_up), join(full_down)
    full_qkv, full_out = full_attend[:, :3 * cols], full_attend[:, 3 * cols:]
    bias_qkv = jnp.concatenate([
        lax.dynamic_slice_in_dim(bias_query, tensor * cols, cols),
        jnp.zeros((cols,), F32),
        lax.dynamic_slice_in_dim(bias_value, tensor * cols, cols),
    ])
    up_bias = lax.dynamic_slice_in_dim(bias_up, tensor * units, units)
    qkv = (jnp.dot(rows_one, full_qkv, preferred_element_type=F32) + bias_qkv).astype(BF16)
    attended = call(
        functools.partial(attend_kernel, heads, scale), [VM],
        (shape((length, cols)),), [], (qkv,), "attend",
    )[0]
    partial_one = jnp.einsum("tc,dc->td", attended, full_out, preferred_element_type=F32)
    landing = [pltpu.VMEM((3, frames_here, width), BF16), pltpu.VMEM((frames_here, width), BF16)]
    hidden_state, rows_two = call(
        middle_kernel, [VM] * 5,
        [shape((frames_here, width), F32), shape(block)],
        landing + dma(10),
        (partial_one.astype(BF16).reshape(block), inputs, row(bias_out), row(gain_two),
         row(shift_two)),
        "middle", 1,
    )
    rows_two = rows_two.reshape(length, width)
    pre_act = jnp.dot(rows_two, full_up, preferred_element_type=F32) + up_bias
    activated = exact_gelu(pre_act).astype(BF16)
    grad_act = jnp.dot(cots, full_down, preferred_element_type=F32)
    grad_pre = jax.vjp(exact_gelu, pre_act)[1](grad_act)[0]
    grad_up_bias = jnp.sum(grad_pre, axis=0)
    grad_pre_low = grad_pre.astype(BF16)
    back_two = jnp.einsum("tf,df->td", grad_pre_low, full_up, preferred_element_type=F32)
    grad_hidden, rows_hidden, small = call(
        turn_kernel, [VM] * 4,
        [shape((frames_here, width), F32), shape(block), shape((8, width), F32)],
        landing + dma(10),
        (back_two.astype(BF16).reshape(block), hidden_state, cotangent, row(gain_two)),
        "turn", 2,
    )
    rows_hidden = rows_hidden.reshape(length, width)
    partial_two = jnp.einsum("tf,df->td", activated, full_down, preferred_element_type=F32)
    grad_down = jnp.einsum("td,tf->df", cots, activated, preferred_element_type=F32)
    grad_up = jnp.einsum("td,tf->df", rows_two, grad_pre_low, preferred_element_type=F32)
    grad_attended = jnp.dot(rows_hidden, full_out, preferred_element_type=F32).astype(BF16)
    low, bias_sums = call(
        functools.partial(attend_back_kernel, heads, scale), [VM] * 2,
        [shape((length, 3 * cols)), shape((1, 2 * cols), F32)],
        [pltpu.VMEM((length, cols), F32), pltpu.VMEM((heads, HD, length), F32),
         pltpu.VMEM((heads, HD, length), F32)],
        (qkv, grad_attended), "attend_back",
    )
    back_one = jnp.einsum("tc,dc->td", low, full_qkv, preferred_element_type=F32)
    grad_qkv = jnp.einsum("td,tc->dc", rows_one, low, preferred_element_type=F32).astype(BF16)
    grad_out = jnp.einsum("td,tc->dc", rows_hidden, attended, preferred_element_type=F32)
    grad_attend = jnp.concatenate([grad_qkv, grad_out.astype(BF16)], axis=1)
    small = small.at[4, :2 * cols].set(bias_sums[0]).at[5, :units].set(grad_up_bias)
    half = count // 2
    n_copies = 10 + 3 * (2 * half - 1) + half + 3
    output, grad_inputs, sum_attend, sum_up, sum_down, totals = call(
        functools.partial(last_kernel, count), [VM] * 11,
        [shape((frames_here, width), F32), shape((frames_here, width), F32),
         shape((padded, wide), F32), shape((padded, units), F32), shape((padded, units), F32),
         shape((tensors, 8, width), F32)],
        landing + landing
        + [pltpu.VMEM((half, padded, size), BF16) for size in (wide, units, units) * 2]
        + [pltpu.VMEM((8, width), F32), pltpu.VMEM((8, width), F32),
           pltpu.VMEM((half, 8, width), F32), pltpu.VMEM((tensors, 8, width), F32)]
        + dma(n_copies),
        (partial_two.astype(BF16).reshape(block), back_one.astype(BF16).reshape(block),
         hidden_state, row(bias_down), inputs, row(gain_one), grad_hidden, small,
         split(grad_attend), split(grad_up.astype(BF16)), split(grad_down.astype(BF16))),
        "last", 3,
    )
    sums = jnp.sum(totals, axis=0)
    sum_attend = sum_attend[:rows]
    return (
        output,
        grad_inputs,
        sum_attend[:, :cols],
        sum_attend[:, cols:2 * cols],
        sum_attend[:, 2 * cols:3 * cols],
        totals[:, 4, :cols].reshape(-1),
        totals[:, 4, cols:2 * cols].reshape(-1),
        sum_attend[:, 3 * cols:].T,
        sums[2],
        sums[6],
        sums[7],
        sums[0],
        sums[1],
        sum_up[:rows],
        totals[:, 5, :units].reshape(-1),
        sum_down[:rows].T,
        sums[3],
    )


def solution(mesh):
    placed = (
        P(("shard", "tensor"), None),
        P("shard", "tensor"),
        P("shard", "tensor"),
        P("shard", "tensor"),
        P(),
        P(),
        P("tensor", "shard"),
        P(),
        P(),
        P(),
        P(),
        P(),
        P("shard", "tensor"),
        P(),
        P("tensor", "shard"),
        P(),
        P(("shard", "tensor"), None),
    )
    return jax.shard_map(
        shards,
        mesh=mesh,
        in_specs=placed,
        out_specs=(
            P(("shard", "tensor"), None),
            P(("shard", "tensor"), None),
            P("shard", "tensor"),
            P("shard", "tensor"),
            P("shard", "tensor"),
            P(),
            P(),
            P("tensor", "shard"),
            P(),
            P(),
            P(),
            P(),
            P(),
            P("shard", "tensor"),
            P(),
            P("tensor", "shard"),
            P(),
        ),
        check_vma=False,
    )
```

```python
import functools
import math

import jax
import jax.numpy as jnp
from jax import lax
from jax.experimental import pallas as pl
from jax.experimental.pallas import tpu as pltpu
from jax.sharding import PartitionSpec as P

HD = 64
MESH = pl.DeviceIdType.MESH
F32 = jnp.float32
BF16 = jnp.bfloat16

epsilon = 1e-05


def normalize(matrix, gain_vec, shift_vec):
    center = matrix - jnp.mean(matrix, axis=1, keepdims=True)
    inverse = lax.rsqrt(jnp.mean(center * center, axis=1, keepdims=True) + epsilon)
    unit_rows = center * inverse
    return (unit_rows * gain_vec + shift_vec, unit_rows, inverse)


def norm_backward(grad_normed, unit_rows, inverse, gain_vec):
    grad_unit = grad_normed * gain_vec
    first_mean = jnp.mean(grad_unit, axis=1, keepdims=True)
    second_mean = jnp.mean(grad_unit * unit_rows, axis=1, keepdims=True)
    grad_rows = inverse * (grad_unit - first_mean - unit_rows * second_mean)
    return (grad_rows, jnp.sum(grad_normed * unit_rows, axis=0), jnp.sum(grad_normed, axis=0))


def exact_gelu(values):
    return jax.nn.gelu(values, approximate=False)


def flip(index, bit):
    return index + bit - 2 * bit * lax.rem(lax.div(index, bit), 2)


def greet(tensor_peers, shard_peers):
    barrier = pltpu.get_barrier_semaphore()
    for peer in tensor_peers:
        pl.semaphore_signal(barrier, inc=1, device_id={"tensor": peer}, device_id_type=MESH)
    for peer in shard_peers:
        pl.semaphore_signal(barrier, inc=1, device_id={"shard": peer}, device_id_type=MESH)
    pl.semaphore_wait(barrier, len(tensor_peers) + len(shard_peers))


def shard_peers_of(me, count):
    return [flip(me, 1)] + [lax.rem(me + 2 * step, count) for step in range(1, count // 2)]


class Tally:
    def __init__(self, send, recv):
        self.send, self.recv, self.used, self.sent = send, recv, 0, []

    def copy(self, source, target, **peer):
        slot = self.used
        self.used += 1
        made = pltpu.make_async_remote_copy(
            src_ref=source,
            dst_ref=target,
            send_sem=self.send.at[slot],
            recv_sem=self.recv.at[slot],
            device_id=peer,
            device_id_type=MESH,
        )
        made.start()
        self.sent.append(made)
        return made

    def finish(self):
        for made in self.sent:
            made.wait_send()


def halves(rows, parts=2):
    size = rows // parts
    return [pl.ds(part * size, size) for part in range(parts)]


def tensor_gather_start(tally, blocks, tensor):
    rows = blocks.shape[1]
    far = [
        tally.copy(blocks.at[tensor, cut], blocks.at[tensor, cut], tensor=flip(tensor, 2))
        for cut in halves(rows)
    ]
    near = [tally.copy(blocks.at[tensor], blocks.at[tensor], tensor=flip(tensor, 1))]
    return far, near


def tensor_gather_end(tally, blocks, tensor, state):
    far, near = state
    rows = blocks.shape[1]
    other = flip(tensor, 2)
    for arrived, cut in zip(far, halves(rows)):
        arrived.wait_recv()
        near.append(
            tally.copy(blocks.at[other, cut], blocks.at[other, cut], tensor=flip(tensor, 1))
        )
    for arrived in near:
        arrived.wait_recv()


def sum_start_pass(tally, parts, landed, tensor):
    sibling = flip(tensor, 1)
    return [
        tally.copy(parts.at[flip(sibling, 2), cut], landed.at[1, cut], tensor=sibling)
        for cut in halves(parts.shape[1])
    ]


def sum_start_own(tally, parts, landed, tensor):
    sibling = flip(tensor, 1)
    return tally.copy(parts.at[sibling], landed.at[0], tensor=sibling)


def tensor_sum_start(tally, parts, landed, tensor):
    passing = sum_start_pass(tally, parts, landed, tensor)
    return passing, sum_start_own(tally, parts, landed, tensor)


def tensor_sum_pass(tally, parts, landed, mixed, tensor, state):
    far = flip(tensor, 2)
    rows = parts.shape[1]
    across = []
    for arrived, cut in zip(state[0], halves(rows)):
        arrived.wait_recv()
        mixed[cut, :] = (parts[far, cut, :].astype(F32) + landed[1, cut, :].astype(F32)).astype(
            BF16
        )
        across.append(tally.copy(mixed.at[cut], landed.at[2, cut], tensor=far))
    return across


def tensor_sum_end(parts, landed, tensor, state, across):
    state[1].wait_recv()
    for arrived in across:
        arrived.wait_recv()
    return parts[tensor].astype(F32) + landed[0].astype(F32) + landed[2].astype(F32)


def soft_rows(query, keys, scale):
    scores = lax.dot_general(
        query, keys, (((1,), (1,)), ((), ())), preferred_element_type=F32
    ) * scale
    exponent = jnp.exp(scores - jnp.max(scores, axis=1, keepdims=True))
    return exponent * (1.0 / jnp.sum(exponent, axis=1, keepdims=True))


def head_of(ref, rows, head, part, width):
    begin = part * width + head * HD
    return ref[rows, begin:begin + HD]


def front_kernel(count, heads, kept, scale, x_ref, vec_ref, bias_ref, cot_ref, w0, w1, w2,
                 rows_ref, cots_ref, up_ref, down_ref, qkv_w, out_w, qkv_ref, attended_ref,
                 hidden_ref, two_ref, attend_full, parts, landed, mixed, send, recv, local):
    tensor, shard = lax.axis_index("tensor"), lax.axis_index("shard")
    partner = flip(shard, 1)
    peers = shard_peers_of(shard, count)
    greet([flip(tensor, 1), flip(tensor, 2)], peers)
    tally = Tally(send, recv)
    w_refs, full_refs = (w0, w1, w2), (attend_full, up_ref, down_ref)
    keeps = []
    for place, (w_ref, full) in enumerate(zip(w_refs, full_refs)):
        keeps.append(pltpu.make_async_copy(w_ref, full.at[shard], local.at[place]))
    keeps.append(pltpu.make_async_copy(cot_ref, cots_ref.at[tensor], local.at[3]))
    straight, beside = [], []

    def send_own(place):
        w_ref, full = w_refs[place], full_refs[place]
        straight.append([tally.copy(w_ref, full.at[shard], shard=peer) for peer in peers[1:]])
        beside.append(tally.copy(w_ref, full.at[shard], shard=partner))

    passed = [[], [], []]

    def forward(place):
        full = full_refs[place]
        for step in range(1, count // 2):
            straight[place][step - 1].wait_recv()
            origin = lax.rem(shard + count - 2 * step, count)
            passed[place].append(tally.copy(full.at[origin], full.at[origin], shard=partner))

    send_own(0)
    gain_one, shift_one = vec_ref[0:1, :], vec_ref[1:2, :]
    rows_ref[tensor] = normalize(x_ref[...].astype(F32), gain_one, shift_one)[0].astype(BF16)
    rows_state = tensor_gather_start(tally, rows_ref, tensor)
    for keep in keeps:
        keep.start()
    send_own(1)
    send_own(2)
    for keep in keeps:
        keep.wait()
    tensor_gather_end(tally, rows_ref, tensor, rows_state)
    cot_state = tensor_gather_start(tally, cots_ref, tensor)
    forward(0)
    for arrived in beside[:1] + passed[0]:
        arrived.wait_recv()
    width = heads * HD
    for place in range(count):
        into = slice(place * kept, (place + 1) * kept)
        qkv_w[into, :] = attend_full[place, :kept, :3 * width]
        out_w[into, :] = attend_full[place, :kept, 3 * width:]
    size = rows_ref.shape[1]

    def project(step, carry):
        rows = pl.ds(pl.multiple_of(step * size, size), size)
        qkv_ref[rows, :] = (
            jnp.dot(rows_ref[step], qkv_w[...], preferred_element_type=F32) + bias_ref[...]
        ).astype(BF16)
        return carry

    lax.fori_loop(0, rows_ref.shape[0], project, 0)
    everything = slice(None)

    def attend(owner):
        rows = pl.ds(pl.multiple_of(owner * size, size), size)
        blended = []
        for head in range(heads):
            soft = soft_rows(
                head_of(qkv_ref, rows, head, 0, width),
                head_of(qkv_ref, everything, head, 1, width), scale,
            ).astype(BF16)
            values = head_of(qkv_ref, everything, head, 2, width)
            blended.append(jnp.dot(soft, values, preferred_element_type=F32))
        attended = jnp.concatenate(blended, axis=1).astype(BF16)
        attended_ref[rows, :] = attended
        parts[owner] = lax.dot_general(
            attended, out_w[...], (((1,), (1,)), ((), ())), preferred_element_type=F32
        ).astype(BF16)

    sibling, far = flip(tensor, 1), flip(tensor, 2)
    attend(flip(sibling, 2))
    passing = sum_start_pass(tally, parts, landed, tensor)
    attend(far)
    across = tensor_sum_pass(tally, parts, landed, mixed, tensor, (passing, None))
    attend(sibling)
    own = sum_start_own(tally, parts, landed, tensor)
    attend(tensor)
    forward(1)
    branch = tensor_sum_end(parts, landed, tensor, (passing, own), across)
    hidden = x_ref[...].astype(F32) + branch + vec_ref[2:3, :]
    hidden_ref[...] = hidden
    two_ref[tensor] = normalize(hidden, vec_ref[3:4, :], vec_ref[4:5, :])[0].astype(BF16)
    two_state = tensor_gather_start(tally, two_ref, tensor)
    forward(2)
    tensor_gather_end(tally, cots_ref, tensor, cot_state)
    tensor_gather_end(tally, two_ref, tensor, two_state)
    for arrived in beside[1:] + passed[1] + passed[2]:
        arrived.wait_recv()
    tally.finish()


def shard_sum_start(tally, grads, ybufs, shard, count):
    half = count // 2
    place = lax.div(shard, 2)
    low = lax.rem(shard, 2)
    sent = []
    for step in list(range(1, half)) + [0]:
        pair = lax.rem(place + step, half)
        row = []
        for grad, ybuf in zip(grads, ybufs):
            row.append(
                tally.copy(grad.at[pair * 2 + 1 - low], ybuf.at[step], shard=flip(shard, 1))
            )
        sent.append((step, row))
    return sent


def shard_sum_pass(tally, grads, ybufs, zbufs, shard, count, sent):
    half = count // 2
    place = lax.div(shard, 2)
    low = lax.rem(shard, 2)
    across = []
    for step, row in sent:
        pair = lax.rem(place + step, half)
        for grad, ybuf, zbuf, arrived in zip(grads, ybufs, zbufs, row):
            arrived.wait_recv()
            if step:
                ybuf[step] = (
                    grad[pair * 2 + low].astype(F32) + ybuf[step].astype(F32)
                ).astype(BF16)
                across.append(
                    tally.copy(ybuf.at[step], zbuf.at[step], shard=pair * 2 + low)
                )
    return across


def shard_sum_end(grads, ybufs, zbufs, outs, shard, count, across):
    for arrived in across:
        arrived.wait_recv()
    for grad, ybuf, zbuf, out in zip(grads, ybufs, zbufs, outs):
        total = grad[shard].astype(F32) + ybuf[0].astype(F32)
        for step in range(1, count // 2):
            total = total + zbuf[step].astype(F32)
        out[...] = total


def back_kernel(count, heads, kept, scale, back_ref, two_ref, hidden_ref, cot_ref, x_ref,
                vec_ref, qkv_ref, attended_ref, rows_ref, qkv_w, out_w, up_bias, g1, g2,
                output_ref, inputs_ref, o0, o1, o2, total_ref,
                landed0, mixed0, landed2, mixed2, landed1, mixed1, y0, y1, y2, z0, z1, z2,
                grad_ref, rows_hidden, grad_att, dq, dk, dv, low, one_ref, acc_qkv, acc_out, g0,
                mine, sums_t, sums_s, sums_g, send, recv):
    tensor, shard = lax.axis_index("tensor"), lax.axis_index("shard")
    near, far = flip(tensor, 1), flip(tensor, 2)
    partner = flip(shard, 1)
    peers = shard_peers_of(shard, count)
    greet([near, far, flip(near, 2)], peers)
    tally = Tally(send, recv)
    width = heads * HD
    half = count // 2
    size = rows_ref.shape[1]
    blocks = rows_ref.shape[0]
    length = size * blocks
    state = tensor_sum_start(tally, back_ref, landed0, tensor)
    feed, feed_y, feed_z = (g1, g2), (y1, y2), (z1, z2)
    feed_sent = shard_sum_start(tally, feed, feed_y, shard, count)
    across = tensor_sum_pass(tally, back_ref, landed0, mixed0, tensor, state)
    gain_one, gain_two = vec_ref[0:1, :], vec_ref[3:4, :]
    _, unit, inverse = normalize(hidden_ref[...], gain_two, gain_two)
    normed = tensor_sum_end(back_ref, landed0, tensor, state, across)
    grad_rows, grad_gain, grad_shift = norm_backward(normed, unit, inverse, gain_two)
    cot = cot_ref[...].astype(F32)
    grad = cot + grad_rows
    grad_ref[...] = grad
    rows_hidden[tensor] = grad.astype(BF16)
    rows_state = tensor_gather_start(tally, rows_hidden, tensor)
    mine[0:1, :] = grad_gain.reshape(1, -1)
    mine[1:2, :] = grad_shift.reshape(1, -1)
    mine[2:3, :] = jnp.sum(grad, axis=0, keepdims=True)
    mine[3:4, :] = jnp.sum(cot, axis=0, keepdims=True)
    mine[5:6, :] = up_bias[...]
    dk[...] = jnp.zeros_like(dk)
    dv[...] = jnp.zeros_like(dv)
    acc_qkv[...] = jnp.zeros_like(acc_qkv)
    acc_out[...] = jnp.zeros_like(acc_out)
    tensor_gather_end(tally, rows_hidden, tensor, rows_state)
    two_state = tensor_sum_start(tally, two_ref, landed2, tensor)
    feed_across = shard_sum_pass(tally, feed, feed_y, feed_z, shard, count, feed_sent)
    everything = slice(None)
    turned = (((0,), (0,)), ((), ()))
    crossed = (((1,), (1,)), ((), ()))

    def prepare(step, carry):
        rows = pl.ds(pl.multiple_of(step * size, size), size)
        grads = rows_hidden[step]
        grad_att[rows, :] = jnp.dot(grads, out_w[...], preferred_element_type=F32).astype(BF16)
        acc_out[...] += lax.dot_general(
            grads, attended_ref[rows, :], turned, preferred_element_type=F32
        )
        return carry

    lax.fori_loop(0, blocks, prepare, 0)
    two_across = tensor_sum_pass(tally, two_ref, landed2, mixed2, tensor, two_state)

    def block(step, carry):
        rows = pl.ds(pl.multiple_of(step * size, size), size)
        back = []
        for head in range(heads):
            query = head_of(qkv_ref, rows, head, 0, width)
            keys = head_of(qkv_ref, everything, head, 1, width)
            values = head_of(qkv_ref, everything, head, 2, width)
            grad = grad_att[rows, head * HD:(head + 1) * HD]
            soft = soft_rows(query, keys, scale)
            grad_soft = lax.dot_general(grad, values, crossed, preferred_element_type=F32)
            inner = jnp.sum(grad_soft * soft, axis=1, keepdims=True)
            grad_scores = (soft * (grad_soft - inner) * scale).astype(BF16)
            back.append(jnp.dot(grad_scores, keys, preferred_element_type=F32))
            dk[head] += lax.dot_general(query, grad_scores, turned, preferred_element_type=F32)
            dv[head] += lax.dot_general(
                grad, soft.astype(BF16), turned, preferred_element_type=F32
            )
        dq[rows, :] = jnp.concatenate(back, axis=1)
        return carry

    lax.fori_loop(0, blocks, block, 0)
    key_rows = jnp.concatenate([dk[head] for head in range(heads)], axis=0).T
    value_rows = jnp.concatenate([dv[head] for head in range(heads)], axis=0).T
    query_rows = dq[...]
    low[...] = jnp.concatenate([query_rows, key_rows, value_rows], axis=1).astype(BF16)
    mine[4:5, :] = jnp.concatenate(
        [jnp.sum(query_rows, axis=0, keepdims=True), jnp.sum(value_rows, axis=0, keepdims=True),
         jnp.zeros((1, mine.shape[1] - 2 * width), F32)],
        axis=1,
    )

    def spread_back(owner):
        rows = pl.ds(pl.multiple_of(owner * size, size), size)
        one_ref[owner] = lax.dot_general(
            low[rows, :], qkv_w[...], crossed, preferred_element_type=F32
        ).astype(BF16)

    spread_back(flip(near, 2))
    one_pass = sum_start_pass(tally, one_ref, landed1, tensor)
    spread_back(far)
    spread_back(near)
    one_state = (one_pass, sum_start_own(tally, one_ref, landed1, tensor))
    one_across = tensor_sum_pass(tally, one_ref, landed1, mixed1, tensor, one_state)
    spread_back(tensor)

    def weights(step, carry):
        rows = pl.ds(pl.multiple_of(step * size, size), size)
        acc_qkv[...] += lax.dot_general(
            rows_ref[step], low[rows, :], turned, preferred_element_type=F32
        )
        return carry

    lax.fori_loop(0, blocks, weights, 0)
    if kept != g0.shape[1]:
        g0[...] = jnp.zeros_like(g0)
    for place in range(count):
        part = slice(place * kept, (place + 1) * kept)
        g0[place, :kept, :] = jnp.concatenate([acc_qkv[part, :], acc_out[part, :]], axis=1).astype(
            BF16
        )
    sent = shard_sum_start(tally, (g0,), (y0,), shard, count)
    _, unit, inverse = normalize(x_ref[...].astype(F32), gain_one, gain_one)
    normed = tensor_sum_end(one_ref, landed1, tensor, one_state, one_across)
    grad_rows, grad_gain, grad_shift = norm_backward(normed, unit, inverse, gain_one)
    mine[6:7, :] = grad_gain.reshape(1, -1)
    mine[7:8, :] = grad_shift.reshape(1, -1)
    first = tally.copy(mine, sums_s.at[0], shard=partner)
    inputs_ref[...] = grad_ref[...] + grad_rows
    attend_across = shard_sum_pass(tally, (g0,), (y0,), (z0,), shard, count, sent)
    first.wait_recv()
    sums_t[...] = mine[...] + sums_s[0]
    hops = [
        tally.copy(sums_t, sums_s.at[step], shard=lax.rem(shard + 2 * step, count))
        for step in range(1, half)
    ]
    branch = tensor_sum_end(two_ref, landed2, tensor, two_state, two_across)
    output_ref[...] = hidden_ref[...] + branch + vec_ref[5:6, :]
    shard_sum_end(feed, feed_y, feed_z, (o1, o2), shard, count, feed_across)
    for hop in hops:
        hop.wait_recv()
    slot_total = None
    for spot in range(half):
        step = lax.rem(lax.div(shard, 2) + half - spot, half)
        value = jnp.where(step == 0, sums_t[...], sums_s[step])
        slot_total = value if slot_total is None else slot_total + value
    sums_g[tensor] = slot_total
    spread = [
        tally.copy(sums_g.at[tensor], sums_g.at[tensor], tensor=peer)
        for peer in (near, far, flip(near, 2))
    ]
    shard_sum_end((g0,), (y0,), (z0,), (o0,), shard, count, attend_across)
    for arrived in spread:
        arrived.wait_recv()
    total_ref[...] = sums_g[...]
    tally.finish()


def finish_kernel(cols, kept, output_in, inputs_in, attend_in, up_in, down_in, total_in,
                  output_ref, inputs_ref, query_ref, key_ref, value_ref, out_ref, up_ref,
                  down_ref, sum_ref):
    output_ref[...] = output_in[...]
    inputs_ref[...] = inputs_in[...]
    query_ref[...] = attend_in[:kept, :cols]
    key_ref[...] = attend_in[:kept, cols:2 * cols]
    value_ref[...] = attend_in[:kept, 2 * cols:3 * cols]
    out_ref[...] = attend_in[:kept, 3 * cols:].T
    up_ref[...] = up_in[:kept, :]
    down_ref[...] = down_in[:kept, :].T
    sum_ref[...] = jnp.sum(total_in[...], axis=0)


VM = pl.BlockSpec(memory_space=pltpu.VMEM)
HB = pl.BlockSpec(memory_space=pl.ANY)


def call(kernel, ins, outs, scratch, operands, name, collective=None):
    remote = collective is not None
    return pl.pallas_call(
        kernel,
        out_shape=list(outs),
        in_specs=ins,
        out_specs=[VM] * len(outs),
        scratch_shapes=scratch,
        compiler_params=pltpu.CompilerParams(
            vmem_limit_bytes=56 * 2**20,
            **(dict(collective_id=collective, has_side_effects=True) if remote else {}),
        ),
        name=name,
    )(*operands)


def dma(count):
    return [pltpu.SemaphoreType.DMA((count,)), pltpu.SemaphoreType.DMA((count,))]


def shape(dims, kind=BF16):
    return jax.ShapeDtypeStruct(tuple(dims), kind)


def shards(
    inputs, w_query, w_key, w_value, bias_query, bias_value, w_out, bias_out, gain_one,
    shift_one, gain_two, shift_two, w_up, bias_up, w_down, bias_down, cotangent,
):
    count, tensors = lax.axis_size("shard"), lax.axis_size("tensor")
    tensor = lax.axis_index("tensor")
    frames_here, width = inputs.shape
    length = frames_here * tensors
    cols = w_query.shape[1]
    heads = cols // HD
    units = w_up.shape[1]
    scale = 1.0 / math.sqrt(HD)
    rows = w_query.shape[0]
    padded = -(-rows // 16) * 16
    row = lambda vector: vector.reshape(1, -1)
    pad = lambda block: jnp.pad(block, ((0, padded - rows), (0, 0)))
    join = lambda blocks: blocks[:, :rows].reshape(count * rows, blocks.shape[2])
    split = lambda whole: jnp.pad(
        whole.reshape(count, rows, whole.shape[1]), ((0, 0), (0, padded - rows), (0, 0))
    )
    w_attend = jnp.concatenate([w_query, w_key, w_value, w_out.T], axis=1)
    wide = w_attend.shape[1]
    block = (tensors, frames_here, width)
    vectors = jnp.concatenate(
        [gain_one, shift_one, bias_out, gain_two, shift_two, bias_down, gain_one, gain_one]
    ).reshape(8, width)
    bias_qkv = jnp.concatenate([
        lax.dynamic_slice_in_dim(bias_query, tensor * cols, cols),
        jnp.zeros((cols,), F32),
        lax.dynamic_slice_in_dim(bias_value, tensor * cols, cols),
    ])
    up_bias = lax.dynamic_slice_in_dim(bias_up, tensor * units, units)
    landing = [pltpu.VMEM((3, frames_here, width), BF16), pltpu.VMEM((frames_here, width), BF16)]

    n_copies = 5 * 4 + 3 * count
    (rows_one, cots, full_up, full_down, full_qkv, full_out, qkv, attended, hidden_state,
     rows_two) = call(
        functools.partial(front_kernel, count, heads, rows, scale),
        [VM] * 7,
        [shape(block), shape(block), shape((count, padded, units)),
         shape((count, padded, units)), shape((width, 3 * cols)), shape((width, cols)),
         shape((length, 3 * cols)), shape((length, cols)), shape((frames_here, width), F32),
         shape(block)],
        [pltpu.VMEM((count, padded, wide), BF16), pltpu.VMEM(block, BF16)] + landing
        + dma(n_copies) + [pltpu.SemaphoreType.DMA((4,))],
        (inputs, vectors, row(bias_qkv), cotangent, pad(w_attend), pad(w_up), pad(w_down.T)),
        "front", 0,
    )
    cots = cots.reshape(length, width)
    rows_two = rows_two.reshape(length, width)
    full_up, full_down = join(full_up), join(full_down)
    pre_act = jnp.dot(rows_two, full_up, preferred_element_type=F32) + up_bias
    activated = exact_gelu(pre_act).astype(BF16)
    grad_act = jnp.dot(cots, full_down, preferred_element_type=F32)
    grad_pre = jax.vjp(exact_gelu, pre_act)[1](grad_act)[0]
    grad_up_bias = jnp.sum(grad_pre, axis=0)
    grad_pre_low = grad_pre.astype(BF16)
    back_two = jnp.einsum("tf,df->td", grad_pre_low, full_up, preferred_element_type=F32)
    partial_two = jnp.einsum("tf,df->td", activated, full_down, preferred_element_type=F32)
    grad_down = jnp.einsum("td,tf->df", cots, activated, preferred_element_type=F32)
    grad_up = jnp.einsum("td,tf->df", rows_two, grad_pre_low, preferred_element_type=F32)
    half = count // 2
    n_copies = 5 * 4 + 3 * (2 * half - 1) + half + 3
    output, grad_inputs, sum_attend, sum_up, sum_down, totals = call(
        functools.partial(back_kernel, count, heads, rows, scale), [VM] * 14,
        [shape((frames_here, width), F32), shape((frames_here, width), F32),
         shape((padded, wide), F32), shape((padded, units), F32), shape((padded, units), F32),
         shape((tensors, 8, width), F32)],
        landing * 3
        + [pltpu.VMEM((half, padded, size), BF16) for size in (wide, units, units) * 2]
        + [pltpu.VMEM((frames_here, width), F32), pltpu.VMEM(block, BF16),
           pltpu.VMEM((length, cols), BF16), pltpu.VMEM((length, cols), F32),
           pltpu.VMEM((heads, HD, length), F32), pltpu.VMEM((heads, HD, length), F32),
           pltpu.VMEM((length, 3 * cols), BF16), pltpu.VMEM(block, BF16),
           pltpu.VMEM((width, 3 * cols), F32), pltpu.VMEM((width, cols), F32),
           pltpu.VMEM((count, padded, wide), BF16),
           pltpu.VMEM((8, width), F32), pltpu.VMEM((8, width), F32),
           pltpu.VMEM((half, 8, width), F32), pltpu.VMEM((tensors, 8, width), F32)]
        + dma(n_copies),
        (back_two.astype(BF16).reshape(block), partial_two.astype(BF16).reshape(block),
         hidden_state, cotangent, inputs, vectors, qkv, attended, rows_one, full_qkv, full_out,
         row(grad_up_bias), split(grad_up.astype(BF16)), split(grad_down.astype(BF16))),
        "back", 1,
    )
    (output, grad_inputs, grad_query, grad_key, grad_value, grad_w_out, grad_w_up, grad_w_down,
     sums) = call(
        functools.partial(finish_kernel, cols, rows), [VM] * 6,
        [shape((frames_here, width), F32), shape((frames_here, width), F32)]
        + [shape((rows, cols), F32)] * 3
        + [shape((cols, rows), F32), shape((rows, units), F32), shape((units, rows), F32),
           shape((8, width), F32)],
        [], (output, grad_inputs, sum_attend, sum_up, sum_down, totals), "finish",
    )
    return (
        output,
        grad_inputs,
        grad_query,
        grad_key,
        grad_value,
        totals[:, 4, :cols].reshape(-1),
        totals[:, 4, cols:2 * cols].reshape(-1),
        grad_w_out,
        sums[2],
        sums[6],
        sums[7],
        sums[0],
        sums[1],
        grad_w_up,
        totals[:, 5, :units].reshape(-1),
        grad_w_down,
        sums[3],
    )


def solution(mesh):
    placed = (
        P(("shard", "tensor"), None),
        P("shard", "tensor"),
        P("shard", "tensor"),
        P("shard", "tensor"),
        P(),
        P(),
        P("tensor", "shard"),
        P(),
        P(),
        P(),
        P(),
        P(),
        P("shard", "tensor"),
        P(),
        P("tensor", "shard"),
        P(),
        P(("shard", "tensor"), None),
    )
    return jax.shard_map(
        shards,
        mesh=mesh,
        in_specs=placed,
        out_specs=(
            P(("shard", "tensor"), None),
            P(("shard", "tensor"), None),
            P("shard", "tensor"),
            P("shard", "tensor"),
            P("shard", "tensor"),
            P(),
            P(),
            P("tensor", "shard"),
            P(),
            P(),
            P(),
            P(),
            P(),
            P("shard", "tensor"),
            P(),
            P("tensor", "shard"),
            P(),
        ),
        check_vma=False,
    )
```

```python
import functools
import math

import jax
import jax.numpy as jnp
from jax import lax
from jax.experimental import pallas as pl
from jax.experimental.pallas import tpu as pltpu
from jax.sharding import PartitionSpec as P

HD = 64
MESH = pl.DeviceIdType.MESH
F32 = jnp.float32
BF16 = jnp.bfloat16

epsilon = 1e-05


def normalize(matrix, gain_vec, shift_vec):
    center = matrix - jnp.mean(matrix, axis=1, keepdims=True)
    inverse = lax.rsqrt(jnp.mean(center * center, axis=1, keepdims=True) + epsilon)
    unit_rows = center * inverse
    return (unit_rows * gain_vec + shift_vec, unit_rows, inverse)


def norm_backward(grad_normed, unit_rows, inverse, gain_vec):
    grad_unit = grad_normed * gain_vec
    first_mean = jnp.mean(grad_unit, axis=1, keepdims=True)
    second_mean = jnp.mean(grad_unit * unit_rows, axis=1, keepdims=True)
    grad_rows = inverse * (grad_unit - first_mean - unit_rows * second_mean)
    return (grad_rows, jnp.sum(grad_normed * unit_rows, axis=0), jnp.sum(grad_normed, axis=0))


def exact_gelu(values):
    return jax.nn.gelu(values, approximate=False)


def flip(index, bit):
    return index + bit - 2 * bit * lax.rem(lax.div(index, bit), 2)


def greet(tensor_peers, shard_peers):
    barrier = pltpu.get_barrier_semaphore()
    for peer in tensor_peers:
        pl.semaphore_signal(barrier, inc=1, device_id={"tensor": peer}, device_id_type=MESH)
    for peer in shard_peers:
        pl.semaphore_signal(barrier, inc=1, device_id={"shard": peer}, device_id_type=MESH)
    pl.semaphore_wait(barrier, len(tensor_peers) + len(shard_peers))


def shard_peers_of(me, count):
    return [flip(me, 1)] + [lax.rem(me + 2 * step, count) for step in range(1, count // 2)]


class Tally:
    def __init__(self, send, recv):
        self.send, self.recv, self.used, self.sent = send, recv, 0, []

    def copy(self, source, target, **peer):
        slot = self.used
        self.used += 1
        made = pltpu.make_async_remote_copy(
            src_ref=source,
            dst_ref=target,
            send_sem=self.send.at[slot],
            recv_sem=self.recv.at[slot],
            device_id=peer,
            device_id_type=MESH,
        )
        made.start()
        self.sent.append(made)
        return made

    def finish(self):
        for made in self.sent:
            made.wait_send()


def halves(rows, parts=2):
    size = rows // parts
    return [pl.ds(part * size, size) for part in range(parts)]


def tensor_gather_start(tally, blocks, tensor):
    rows = blocks.shape[1]
    far = [
        tally.copy(blocks.at[tensor, cut], blocks.at[tensor, cut], tensor=flip(tensor, 2))
        for cut in halves(rows)
    ]
    near = [tally.copy(blocks.at[tensor], blocks.at[tensor], tensor=flip(tensor, 1))]
    return far, near


def tensor_gather_end(tally, blocks, tensor, state):
    far, near = state
    rows = blocks.shape[1]
    other = flip(tensor, 2)
    for arrived, cut in zip(far, halves(rows)):
        arrived.wait_recv()
        near.append(
            tally.copy(blocks.at[other, cut], blocks.at[other, cut], tensor=flip(tensor, 1))
        )
    for arrived in near:
        arrived.wait_recv()


def sum_start_pass(tally, parts, landed, tensor):
    sibling = flip(tensor, 1)
    return [
        tally.copy(parts.at[flip(sibling, 2), cut], landed.at[1, cut], tensor=sibling)
        for cut in halves(parts.shape[1])
    ]


def sum_start_own(tally, parts, landed, tensor):
    sibling = flip(tensor, 1)
    return tally.copy(parts.at[sibling], landed.at[0], tensor=sibling)


def tensor_sum_start(tally, parts, landed, tensor):
    passing = sum_start_pass(tally, parts, landed, tensor)
    return passing, sum_start_own(tally, parts, landed, tensor)


def tensor_sum_pass(tally, parts, landed, mixed, tensor, state):
    far = flip(tensor, 2)
    rows = parts.shape[1]
    across = []
    for arrived, cut in zip(state[0], halves(rows)):
        arrived.wait_recv()
        mixed[cut, :] = (parts[far, cut, :].astype(F32) + landed[1, cut, :].astype(F32)).astype(
            BF16
        )
        across.append(tally.copy(mixed.at[cut], landed.at[2, cut], tensor=far))
    return across


def tensor_sum_end(parts, landed, tensor, state, across):
    state[1].wait_recv()
    for arrived in across:
        arrived.wait_recv()
    return parts[tensor].astype(F32) + landed[0].astype(F32) + landed[2].astype(F32)


def soft_rows(query, keys, scale):
    scores = lax.dot_general(
        query, keys, (((1,), (1,)), ((), ())), preferred_element_type=F32
    ) * scale
    exponent = jnp.exp(scores - jnp.max(scores, axis=1, keepdims=True))
    return exponent * (1.0 / jnp.sum(exponent, axis=1, keepdims=True))


def head_of(ref, rows, head, part, width):
    begin = part * width + head * HD
    return ref[rows, begin:begin + HD]


def front_kernel(count, heads, kept, scale, x_ref, gain_a, shift_a, bias_o, gain_b, shift_b,
                 bias_q, bias_v, bias_u, cot_ref, w0, w1, w2, up_row, rows_ref, cots_ref, up_ref, down_ref, qkv_w, out_w, qkv_ref, attended_ref,
                 hidden_ref, two_ref, attend_full, parts, landed, mixed, vec_ref, bias_ref,
                 send, recv, local):
    tensor, shard = lax.axis_index("tensor"), lax.axis_index("shard")
    partner = flip(shard, 1)
    peers = shard_peers_of(shard, count)
    greet([flip(tensor, 1), flip(tensor, 2)], peers)
    tally = Tally(send, recv)
    w_refs, full_refs = (w0, w1, w2), (attend_full, up_ref, down_ref)
    keeps = []
    for place, (w_ref, full) in enumerate(zip(w_refs, full_refs)):
        keeps.append(pltpu.make_async_copy(w_ref, full.at[shard], local.at[place]))
    keeps.append(pltpu.make_async_copy(cot_ref, cots_ref.at[tensor], local.at[3]))
    straight, beside = [], []

    def send_own(place):
        w_ref, full = w_refs[place], full_refs[place]
        straight.append([tally.copy(w_ref, full.at[shard], shard=peer) for peer in peers[1:]])
        beside.append(tally.copy(w_ref, full.at[shard], shard=partner))

    passed = [[], [], []]

    def forward(place):
        full = full_refs[place]
        for step in range(1, count // 2):
            straight[place][step - 1].wait_recv()
            origin = lax.rem(shard + count - 2 * step, count)
            passed[place].append(tally.copy(full.at[origin], full.at[origin], shard=partner))

    send_own(0)
    for place, vector in enumerate((gain_a, shift_a, bias_o, gain_b, shift_b)):
        vec_ref[place:place + 1, :] = vector[...].reshape(1, -1)
    blocks = rows_ref.shape[0]

    def own_part(vector):
        whole = vector[...].reshape(1, -1)
        size = whole.shape[1] // blocks
        part = whole[:, :size]
        for place in range(1, blocks):
            part = jnp.where(tensor == place, whole[:, place * size:(place + 1) * size], part)
        return part

    query_part, value_part = own_part(bias_q), own_part(bias_v)
    bias_ref[...] = jnp.concatenate(
        [query_part, jnp.zeros_like(query_part), value_part], axis=1
    )
    up_row[...] = own_part(bias_u)
    gain_one, shift_one = vec_ref[0:1, :], vec_ref[1:2, :]
    rows_ref[tensor] = normalize(x_ref[...].astype(F32), gain_one, shift_one)[0].astype(BF16)
    rows_state = tensor_gather_start(tally, rows_ref, tensor)
    for keep in keeps:
        keep.start()
    for keep in keeps:
        keep.wait()
    tensor_gather_end(tally, rows_ref, tensor, rows_state)
    forward(0)
    send_own(1)
    send_own(2)
    cot_state = tensor_gather_start(tally, cots_ref, tensor)
    for arrived in beside[:1] + passed[0]:
        arrived.wait_recv()
    width = heads * HD
    for place in range(count):
        into = slice(place * kept, (place + 1) * kept)
        qkv_w[into, :] = attend_full[place, :kept, :3 * width]
        out_w[into, :] = attend_full[place, :kept, 3 * width:]
    size = rows_ref.shape[1]

    def project(step, carry):
        rows = pl.ds(pl.multiple_of(step * size, size), size)
        qkv_ref[rows, :] = (
            jnp.dot(rows_ref[step], qkv_w[...], preferred_element_type=F32) + bias_ref[...]
        ).astype(BF16)
        return carry

    lax.fori_loop(0, rows_ref.shape[0], project, 0)
    everything = slice(None)

    def attend(owner):
        rows = pl.ds(pl.multiple_of(owner * size, size), size)
        blended = []
        for head in range(heads):
            soft = soft_rows(
                head_of(qkv_ref, rows, head, 0, width),
                head_of(qkv_ref, everything, head, 1, width), scale,
            ).astype(BF16)
            values = head_of(qkv_ref, everything, head, 2, width)
            blended.append(jnp.dot(soft, values, preferred_element_type=F32))
        attended = jnp.concatenate(blended, axis=1).astype(BF16)
        attended_ref[rows, :] = attended
        parts[owner] = lax.dot_general(
            attended, out_w[...], (((1,), (1,)), ((), ())), preferred_element_type=F32
        ).astype(BF16)

    sibling, far = flip(tensor, 1), flip(tensor, 2)
    attend(flip(sibling, 2))
    passing = sum_start_pass(tally, parts, landed, tensor)
    attend(far)
    across = tensor_sum_pass(tally, parts, landed, mixed, tensor, (passing, None))
    attend(sibling)
    own = sum_start_own(tally, parts, landed, tensor)
    attend(tensor)
    forward(1)
    branch = tensor_sum_end(parts, landed, tensor, (passing, own), across)
    hidden = x_ref[...].astype(F32) + branch + vec_ref[2:3, :]
    hidden_ref[...] = hidden
    two_ref[tensor] = normalize(hidden, vec_ref[3:4, :], vec_ref[4:5, :])[0].astype(BF16)
    two_state = tensor_gather_start(tally, two_ref, tensor)
    forward(2)
    tensor_gather_end(tally, cots_ref, tensor, cot_state)
    tensor_gather_end(tally, two_ref, tensor, two_state)
    for arrived in beside[1:] + passed[1] + passed[2]:
        arrived.wait_recv()
    tally.finish()


def shard_sum_start(tally, grads, ybufs, shard, count):
    half = count // 2
    place = lax.div(shard, 2)
    low = lax.rem(shard, 2)
    sent = []
    for step in list(range(1, half)) + [0]:
        pair = lax.rem(place + step, half)
        row = []
        for grad, ybuf in zip(grads, ybufs):
            row.append(
                tally.copy(grad.at[pair * 2 + 1 - low], ybuf.at[step], shard=flip(shard, 1))
            )
        sent.append((step, row))
    return sent


def shard_sum_pass(tally, grads, ybufs, zbufs, shard, count, sent):
    half = count // 2
    place = lax.div(shard, 2)
    low = lax.rem(shard, 2)
    across = []
    for step, row in sent:
        pair = lax.rem(place + step, half)
        for grad, ybuf, zbuf, arrived in zip(grads, ybufs, zbufs, row):
            arrived.wait_recv()
            if step:
                ybuf[step] = (
                    grad[pair * 2 + low].astype(F32) + ybuf[step].astype(F32)
                ).astype(BF16)
                across.append(
                    tally.copy(ybuf.at[step], zbuf.at[step], shard=pair * 2 + low)
                )
    return across


def shard_sum_end(grads, ybufs, zbufs, outs, shard, count, across):
    for arrived in across:
        arrived.wait_recv()
    for grad, ybuf, zbuf, out in zip(grads, ybufs, zbufs, outs):
        total = grad[shard].astype(F32) + ybuf[0].astype(F32)
        for step in range(1, count // 2):
            total = total + zbuf[step].astype(F32)
        out[...] = total


def back_kernel(count, heads, kept, scale, back_ref, two_ref, hidden_ref, cot_ref, x_ref,
                gain_a, gain_b, bias_d, qkv_ref, attended_ref, rows_ref, qkv_w, out_w, up_bias, g1, g2,
                output_ref, inputs_ref, o0, o1, o2, total_ref,
                landed0, mixed0, landed2, mixed2, landed1, mixed1, y0, y1, y2, z0, z1, z2,
                grad_ref, rows_hidden, grad_att, dq, dk, dv, low, one_ref, acc_qkv, acc_out, g0,
                mine, sums_t, sums_s, sums_g, send, recv):
    tensor, shard = lax.axis_index("tensor"), lax.axis_index("shard")
    near, far = flip(tensor, 1), flip(tensor, 2)
    partner = flip(shard, 1)
    peers = shard_peers_of(shard, count)
    greet([near, far, flip(near, 2)], peers)
    tally = Tally(send, recv)
    width = heads * HD
    half = count // 2
    size = rows_ref.shape[1]
    blocks = rows_ref.shape[0]
    length = size * blocks
    state = tensor_sum_start(tally, back_ref, landed0, tensor)
    feed, feed_y, feed_z = (g1, g2), (y1, y2), (z1, z2)
    feed_sent = shard_sum_start(tally, feed, feed_y, shard, count)
    across = tensor_sum_pass(tally, back_ref, landed0, mixed0, tensor, state)
    gain_one, gain_two = gain_a[...].reshape(1, -1), gain_b[...].reshape(1, -1)
    _, unit, inverse = normalize(hidden_ref[...], gain_two, gain_two)
    normed = tensor_sum_end(back_ref, landed0, tensor, state, across)
    grad_rows, grad_gain, grad_shift = norm_backward(normed, unit, inverse, gain_two)
    cot = cot_ref[...].astype(F32)
    grad = cot + grad_rows
    grad_ref[...] = grad
    rows_hidden[tensor] = grad.astype(BF16)
    rows_state = tensor_gather_start(tally, rows_hidden, tensor)
    mine[0:1, :] = grad_gain.reshape(1, -1)
    mine[1:2, :] = grad_shift.reshape(1, -1)
    mine[2:3, :] = jnp.sum(grad, axis=0, keepdims=True)
    mine[3:4, :] = jnp.sum(cot, axis=0, keepdims=True)
    mine[5:6, :] = up_bias[...]
    dk[...] = jnp.zeros_like(dk)
    dv[...] = jnp.zeros_like(dv)
    acc_qkv[...] = jnp.zeros_like(acc_qkv)
    acc_out[...] = jnp.zeros_like(acc_out)
    tensor_gather_end(tally, rows_hidden, tensor, rows_state)
    two_state = tensor_sum_start(tally, two_ref, landed2, tensor)
    feed_across = shard_sum_pass(tally, feed, feed_y, feed_z, shard, count, feed_sent)
    everything = slice(None)
    turned = (((0,), (0,)), ((), ()))
    crossed = (((1,), (1,)), ((), ()))

    def prepare(step, carry):
        rows = pl.ds(pl.multiple_of(step * size, size), size)
        grads = rows_hidden[step]
        grad_att[rows, :] = jnp.dot(grads, out_w[...], preferred_element_type=F32).astype(BF16)
        acc_out[...] += lax.dot_general(
            grads, attended_ref[rows, :], turned, preferred_element_type=F32
        )
        return carry

    lax.fori_loop(0, blocks, prepare, 0)
    two_across = tensor_sum_pass(tally, two_ref, landed2, mixed2, tensor, two_state)

    def block(step, carry):
        rows = pl.ds(pl.multiple_of(step * size, size), size)
        back = []
        for head in range(heads):
            query = head_of(qkv_ref, rows, head, 0, width)
            keys = head_of(qkv_ref, everything, head, 1, width)
            values = head_of(qkv_ref, everything, head, 2, width)
            grad = grad_att[rows, head * HD:(head + 1) * HD]
            soft = soft_rows(query, keys, scale)
            grad_soft = lax.dot_general(grad, values, crossed, preferred_element_type=F32)
            inner = jnp.sum(grad_soft * soft, axis=1, keepdims=True)
            grad_scores = (soft * (grad_soft - inner) * scale).astype(BF16)
            back.append(jnp.dot(grad_scores, keys, preferred_element_type=F32))
            dk[head] += lax.dot_general(query, grad_scores, turned, preferred_element_type=F32)
            dv[head] += lax.dot_general(
                grad, soft.astype(BF16), turned, preferred_element_type=F32
            )
        dq[rows, :] = jnp.concatenate(back, axis=1)
        return carry

    lax.fori_loop(0, blocks, block, 0)
    key_rows = jnp.concatenate([dk[head] for head in range(heads)], axis=0).T
    value_rows = jnp.concatenate([dv[head] for head in range(heads)], axis=0).T
    query_rows = dq[...]
    low[...] = jnp.concatenate([query_rows, key_rows, value_rows], axis=1).astype(BF16)
    mine[4:5, :] = jnp.concatenate(
        [jnp.sum(query_rows, axis=0, keepdims=True), jnp.sum(value_rows, axis=0, keepdims=True),
         jnp.zeros((1, mine.shape[1] - 2 * width), F32)],
        axis=1,
    )

    def spread_back(owner):
        rows = pl.ds(pl.multiple_of(owner * size, size), size)
        one_ref[owner] = lax.dot_general(
            low[rows, :], qkv_w[...], crossed, preferred_element_type=F32
        ).astype(BF16)

    spread_back(flip(near, 2))
    one_pass = sum_start_pass(tally, one_ref, landed1, tensor)
    spread_back(far)
    spread_back(near)
    one_state = (one_pass, sum_start_own(tally, one_ref, landed1, tensor))
    one_across = tensor_sum_pass(tally, one_ref, landed1, mixed1, tensor, one_state)
    spread_back(tensor)

    def weights(step, carry):
        rows = pl.ds(pl.multiple_of(step * size, size), size)
        acc_qkv[...] += lax.dot_general(
            rows_ref[step], low[rows, :], turned, preferred_element_type=F32
        )
        return carry

    lax.fori_loop(0, blocks, weights, 0)
    if kept != g0.shape[1]:
        g0[...] = jnp.zeros_like(g0)
    for place in range(count):
        part = slice(place * kept, (place + 1) * kept)
        g0[place, :kept, :] = jnp.concatenate([acc_qkv[part, :], acc_out[part, :]], axis=1).astype(
            BF16
        )
    sent = shard_sum_start(tally, (g0,), (y0,), shard, count)
    _, unit, inverse = normalize(x_ref[...].astype(F32), gain_one, gain_one)
    normed = tensor_sum_end(one_ref, landed1, tensor, one_state, one_across)
    grad_rows, grad_gain, grad_shift = norm_backward(normed, unit, inverse, gain_one)
    mine[6:7, :] = grad_gain.reshape(1, -1)
    mine[7:8, :] = grad_shift.reshape(1, -1)
    first = tally.copy(mine, sums_s.at[0], shard=partner)
    inputs_ref[...] = grad_ref[...] + grad_rows
    attend_across = shard_sum_pass(tally, (g0,), (y0,), (z0,), shard, count, sent)
    first.wait_recv()
    sums_t[...] = mine[...] + sums_s[0]
    hops = [
        tally.copy(sums_t, sums_s.at[step], shard=lax.rem(shard + 2 * step, count))
        for step in range(1, half)
    ]
    branch = tensor_sum_end(two_ref, landed2, tensor, two_state, two_across)
    output_ref[...] = hidden_ref[...] + branch + bias_d[...].reshape(1, -1)
    shard_sum_end(feed, feed_y, feed_z, (o1, o2), shard, count, feed_across)
    for hop in hops:
        hop.wait_recv()
    slot_total = None
    for spot in range(half):
        step = lax.rem(lax.div(shard, 2) + half - spot, half)
        value = jnp.where(step == 0, sums_t[...], sums_s[step])
        slot_total = value if slot_total is None else slot_total + value
    sums_g[tensor] = slot_total
    spread = [
        tally.copy(sums_g.at[tensor], sums_g.at[tensor], tensor=peer)
        for peer in (near, far, flip(near, 2))
    ]
    shard_sum_end((g0,), (y0,), (z0,), (o0,), shard, count, attend_across)
    for arrived in spread:
        arrived.wait_recv()
    total_ref[...] = sums_g[...]
    tally.finish()


def finish_kernel(cols, kept, output_in, inputs_in, attend_in, up_in, down_in, total_in,
                  output_ref, inputs_ref, query_ref, key_ref, value_ref, out_ref, up_ref,
                  down_ref, query_b, value_b, bias_o, gain_a, shift_a, gain_b, shift_b, bias_u,
                  bias_d):
    output_ref[...] = output_in[...]
    inputs_ref[...] = inputs_in[...]
    query_ref[...] = attend_in[:kept, :cols]
    key_ref[...] = attend_in[:kept, cols:2 * cols]
    value_ref[...] = attend_in[:kept, 2 * cols:3 * cols]
    out_ref[...] = attend_in[:kept, 3 * cols:].T
    up_ref[...] = up_in[:kept, :]
    down_ref[...] = down_in[:kept, :]
    sums = jnp.sum(total_in[...], axis=0)
    for ref, place in ((gain_b, 0), (shift_b, 1), (bias_o, 2), (bias_d, 3), (gain_a, 6),
                       (shift_a, 7)):
        ref[...] = sums[place:place + 1, :].reshape(-1)
    tensors = total_in.shape[0]
    units = up_in.shape[1]
    for ref, place, begin, size in ((query_b, 4, 0, cols), (value_b, 4, cols, cols),
                                    (bias_u, 5, 0, units)):
        ref[...] = jnp.concatenate(
            [total_in[spot, place:place + 1, begin:begin + size] for spot in range(tensors)],
            axis=1,
        ).reshape(-1)


VM = pl.BlockSpec(memory_space=pltpu.VMEM)
HB = pl.BlockSpec(memory_space=pl.ANY)


def call(kernel, ins, outs, scratch, operands, name, collective=None):
    remote = collective is not None
    return pl.pallas_call(
        kernel,
        out_shape=list(outs),
        in_specs=ins,
        out_specs=[VM] * len(outs),
        scratch_shapes=scratch,
        compiler_params=pltpu.CompilerParams(
            vmem_limit_bytes=56 * 2**20,
            **(dict(collective_id=collective, has_side_effects=True) if remote else {}),
        ),
        name=name,
    )(*operands)


def dma(count):
    return [pltpu.SemaphoreType.DMA((count,)), pltpu.SemaphoreType.DMA((count,))]


def shape(dims, kind=BF16):
    return jax.ShapeDtypeStruct(tuple(dims), kind)


def shards(
    inputs, w_query, w_key, w_value, bias_query, bias_value, w_out, bias_out, gain_one,
    shift_one, gain_two, shift_two, w_up, bias_up, w_down, bias_down, cotangent,
):
    count, tensors = lax.axis_size("shard"), lax.axis_size("tensor")
    tensor = lax.axis_index("tensor")
    frames_here, width = inputs.shape
    length = frames_here * tensors
    cols = w_query.shape[1]
    heads = cols // HD
    units = w_up.shape[1]
    scale = 1.0 / math.sqrt(HD)
    rows = w_query.shape[0]
    padded = -(-rows // 16) * 16
    row = lambda vector: vector.reshape(1, -1)
    pad = lambda block: jnp.pad(block, ((0, padded - rows), (0, 0)))
    join = lambda blocks: blocks[:, :rows].reshape(count * rows, blocks.shape[2])
    split = lambda whole: jnp.pad(
        whole.reshape(count, rows, whole.shape[1]), ((0, 0), (0, padded - rows), (0, 0))
    )
    w_attend = jnp.concatenate([w_query, w_key, w_value, w_out.T], axis=1)
    wide = w_attend.shape[1]
    block = (tensors, frames_here, width)
    landing = [pltpu.VMEM((3, frames_here, width), BF16), pltpu.VMEM((frames_here, width), BF16)]

    n_copies = 5 * 4 + 3 * count
    (up_bias, rows_one, cots, full_up, full_down, full_qkv, full_out, qkv, attended, hidden_state,
     rows_two) = call(
        functools.partial(front_kernel, count, heads, rows, scale),
        [VM] * 13,
        [shape((1, units), F32), shape(block), shape(block), shape((count, padded, units)),
         shape((count, padded, units)), shape((width, 3 * cols)), shape((width, cols)),
         shape((length, 3 * cols)), shape((length, cols)), shape((frames_here, width), F32),
         shape(block)],
        [pltpu.VMEM((count, padded, wide), BF16), pltpu.VMEM(block, BF16)] + landing
        + [pltpu.VMEM((8, width), F32), pltpu.VMEM((1, 3 * cols), F32)]
        + dma(n_copies) + [pltpu.SemaphoreType.DMA((4,))],
        (inputs, gain_one, shift_one, bias_out, gain_two, shift_two, bias_query, bias_value,
         bias_up, cotangent, pad(w_attend), pad(w_up), pad(w_down.T)),
        "front", 0,
    )
    cots = cots.reshape(length, width)
    rows_two = rows_two.reshape(length, width)
    full_up, full_down = join(full_up), join(full_down)
    pre_act = jnp.dot(rows_two, full_up, preferred_element_type=F32) + up_bias
    activated = exact_gelu(pre_act).astype(BF16)
    grad_act = jnp.dot(cots, full_down, preferred_element_type=F32)
    grad_pre = jax.vjp(exact_gelu, pre_act)[1](grad_act)[0]
    grad_up_bias = jnp.sum(grad_pre, axis=0)
    grad_pre_low = grad_pre.astype(BF16)
    back_two = jnp.einsum("tf,df->td", grad_pre_low, full_up, preferred_element_type=F32)
    partial_two = jnp.einsum("tf,df->td", activated, full_down, preferred_element_type=F32)
    grad_down = jnp.einsum("td,tf->df", cots, activated, preferred_element_type=F32)
    grad_up = jnp.einsum("td,tf->df", rows_two, grad_pre_low, preferred_element_type=F32)
    half = count // 2
    n_copies = 5 * 4 + 3 * (2 * half - 1) + half + 3
    output, grad_inputs, sum_attend, sum_up, sum_down, totals = call(
        functools.partial(back_kernel, count, heads, rows, scale), [VM] * 16,
        [shape((frames_here, width), F32), shape((frames_here, width), F32),
         shape((padded, wide), F32), shape((padded, units), F32), shape((padded, units), F32),
         shape((tensors, 8, width), F32)],
        landing * 3
        + [pltpu.VMEM((half, padded, size), BF16) for size in (wide, units, units) * 2]
        + [pltpu.VMEM((frames_here, width), F32), pltpu.VMEM(block, BF16),
           pltpu.VMEM((length, cols), BF16), pltpu.VMEM((length, cols), F32),
           pltpu.VMEM((heads, HD, length), F32), pltpu.VMEM((heads, HD, length), F32),
           pltpu.VMEM((length, 3 * cols), BF16), pltpu.VMEM(block, BF16),
           pltpu.VMEM((width, 3 * cols), F32), pltpu.VMEM((width, cols), F32),
           pltpu.VMEM((count, padded, wide), BF16),
           pltpu.VMEM((8, width), F32), pltpu.VMEM((8, width), F32),
           pltpu.VMEM((half, 8, width), F32), pltpu.VMEM((tensors, 8, width), F32)]
        + dma(n_copies),
        (back_two.astype(BF16).reshape(block), partial_two.astype(BF16).reshape(block),
         hidden_state, cotangent, inputs, gain_one, gain_two, bias_down, qkv, attended, rows_one, full_qkv, full_out,
         row(grad_up_bias), split(grad_up.astype(BF16)), split(grad_down.astype(BF16))),
        "back", 1,
    )
    (output, grad_inputs, grad_query, grad_key, grad_value, grad_w_out, grad_w_up, grad_w_down,
     *sums) = call(
        functools.partial(finish_kernel, cols, rows), [VM] * 6,
        [shape((frames_here, width), F32), shape((frames_here, width), F32)]
        + [shape((rows, cols), F32)] * 3
        + [shape((cols, rows), F32), shape((rows, units), F32), shape((rows, units), F32)]
        + [shape((width,), F32)] * 7 + [shape(bias_up.shape, F32), shape((width,), F32)],
        [], (output, grad_inputs, sum_attend, sum_up, sum_down, totals), "finish",
    )
    (grad_query_bias, grad_value_bias, grad_bias_out, grad_gain_one, grad_shift_one,
     grad_gain_two, grad_shift_two, grad_bias_up, grad_bias_down) = sums
    return (
        output,
        grad_inputs,
        grad_query,
        grad_key,
        grad_value,
        grad_query_bias,
        grad_value_bias,
        grad_w_out,
        grad_bias_out,
        grad_gain_one,
        grad_shift_one,
        grad_gain_two,
        grad_shift_two,
        grad_w_up,
        grad_bias_up,
        grad_w_down.T,
        grad_bias_down,
    )


def solution(mesh):
    placed = (
        P(("shard", "tensor"), None),
        P("shard", "tensor"),
        P("shard", "tensor"),
        P("shard", "tensor"),
        P(),
        P(),
        P("tensor", "shard"),
        P(),
        P(),
        P(),
        P(),
        P(),
        P("shard", "tensor"),
        P(),
        P("tensor", "shard"),
        P(),
        P(("shard", "tensor"), None),
    )
    return jax.shard_map(
        shards,
        mesh=mesh,
        in_specs=placed,
        out_specs=(
            P(("shard", "tensor"), None),
            P(("shard", "tensor"), None),
            P("shard", "tensor"),
            P("shard", "tensor"),
            P("shard", "tensor"),
            P(),
            P(),
            P("tensor", "shard"),
            P(),
            P(),
            P(),
            P(),
            P(),
            P("shard", "tensor"),
            P(),
            P("tensor", "shard"),
            P(),
        ),
        check_vma=False,
    )
```
